512 devices in a mesh: leaf: 32 (over x, y, core), top: 16 (over z).
Axes of the slice: x: 4, y: 4, z: 16, core: 2. Of those that a mesh axis runs over, the one named last changes fastest.
Arguments:
- features: bfloat16 [64, 524288], P(None, ('top', 'leaf')), may hold values from -6 to 6
- lengthscale: float32 [64], replicated, may hold values from 3 to 8
- signal_var: float32 [1], replicated, may hold values from 0.5 to 2
- noise_var: float32 [1], replicated, may hold values from 0.5 to 2
- factors: bfloat16 [8, 524288, 128], P(None, ('top', 'leaf')), may hold values from -3.75 to 4.75
- gains: float32 [8, 128], replicated, may hold values from 6.042172e-06 to 0.00068359375, as said below
- solution: float32 [64, 524288], P(None, ('top', 'leaf')), may hold values from -6 to 6
- residual: float32 [64, 524288], P(None, ('top', 'leaf')), may hold values from -41 to 41
- direction: float32 [64, 524288], P(None, ('top', 'leaf')), may hold values from -41 to 41
Outputs:
- new_solution: float32 [64, 524288], P(None, ('top', 'leaf'))
- new_residual: float32 [64, 524288], P(None, ('top', 'leaf'))
- new_direction: float32 [64, 524288], P(None, ('top', 'leaf'))
The draws below stay inside these ranges and needn't reach their ends.
Inputs may be any that keep to these rules, and one draw needn't show every extreme that they name: gains are positive; the gains of level k lie within a factor of 10 of 0.35 / sqrt(128 * 1024 * 2^k).
All inputs are finite; a program needn't handle non-finite values.
Results may differ from the reference program's by a relative error of at most 0.001.
Values may be sent and summed in bfloat16 or wider, within the bound.
No kernel may reach another device: no remote copies, remote signals or barrier semaphores. Data moves between devices by JAX's collectives and lax.ppermute only.
A program may use at most 64 MiB of HBM per device.

```python
import math
import jax
import jax.numpy as jnp
from jax import lax

F = 64
C = 64
R = 128
LEAF = 2048
PTS_DEV = 1024
LEVELS = 8
POINTS = 524288


def field_scales(key):
    key_chan, key_rows = jax.random.split(key)
    channel = jnp.exp(jax.random.uniform(key_chan, (C, 1), jnp.float32, -0.7, 0.7))
    ramp = jnp.exp(jnp.linspace(math.log(0.6), math.log(1.6), POINTS, dtype=jnp.float32))
    rows = ramp * jnp.exp(jax.random.uniform(key_rows, (POINTS,), jnp.float32, -1.15, 1.15))
    return channel * rows[None, :]


def draw_factors(key, part):
    key = jax.random.fold_in(key, 3)
    key_base, key_offset = jax.random.split(key)
    offset = jax.random.uniform(key_offset, (LEVELS, 1, R), jnp.float32, 0.3, 0.7)
    base = jnp.clip(jax.random.normal(key_base, (LEVELS, POINTS, R), jnp.float32), -4.0, 4.0)
    return (base + offset).astype(jnp.bfloat16)


def draw_gains(key, part):
    key = jax.random.fold_in(key, 5)
    levels = jnp.arange(LEVELS, dtype=jnp.float32) + 1.0
    spread = jnp.exp(jax.random.uniform(key, (LEVELS, R), jnp.float32, math.log(0.1), 0.0))
    return spread * (0.35 / jnp.sqrt(R * PTS_DEV * 2.0 ** levels))[:, None]


def draw_residual(key, part):
    key = jax.random.fold_in(key, 7)
    key_base, key_scale = jax.random.split(key)
    base = jnp.clip(jax.random.normal(key_base, (C, POINTS), jnp.float32), -4.0, 4.0)
    return base * field_scales(key_scale)


def draw_direction(key, part):
    key = jax.random.fold_in(key, 9)
    key_base, key_scale = jax.random.split(key)
    base = jnp.clip(jax.random.normal(key_base, (C, POINTS), jnp.float32), -3.4, 3.4) + 0.6
    return base * field_scales(key_scale)


def steps_of(key, dims, cuts, smallest, largest):
    def one(dim, blocks):
        heights = jax.random.uniform(jax.random.fold_in(jax.random.fold_in(key, 6), dim), (blocks,), jnp.float32, smallest / len(cuts), largest / len(cuts))
        return jnp.repeat(jnp.exp(heights), dims[dim] // blocks).reshape((-1,) + (1,) * (len(dims) - dim - 1))

    gain = one(*cuts[0])
    for cut in cuts[1:]:
        gain = gain * one(*cut)
    return gain


def centred(rng, shape, scale, limit, cuts=(), held_as=jnp.bfloat16):
    array = jax.random.normal(rng, shape, jnp.float32) * scale
    if len(cuts) > 0:
        array = steps_of(rng, shape, cuts, -0.22, 0.18) * array
    return jnp.clip(array, min=-limit, max=limit).astype(held_as)


def setup_inputs(seed: int = 0) -> dict:
    key_list = jax.random.split(jax.random.key(seed), 10)
    features = centred(key_list[0], (F, POINTS), 1.0, 6.0, ((1, 512),))
    lengthscale = jnp.clip(jnp.exp(jax.random.uniform(key_list[1], (F,), jnp.float32, math.log(3.0), math.log(8.0))), 3.0, 8.0)
    signal_var = jnp.clip(jnp.exp(jax.random.uniform(key_list[2], (1,), jnp.float32, math.log(0.5), math.log(2.0))), 0.5, 2.0)
    noise_var = jnp.clip(jnp.exp(jax.random.uniform(key_list[3], (1,), jnp.float32, math.log(0.5), math.log(2.0))), 0.5, 2.0)
    factors = draw_factors(jax.random.fold_in(key_list[9], 71), 0)
    gains = draw_gains(jax.random.fold_in(key_list[9], 71), 0)
    solution = centred(key_list[6], (C, POINTS), 1.0, 6.0, ((1, 512),), jnp.float32)
    residual = draw_residual(jax.random.fold_in(key_list[9], 71), 0)
    direction = draw_direction(jax.random.fold_in(key_list[9], 71), 0)
    return {"features": features, "lengthscale": lengthscale, "signal_var": signal_var, "noise_var": noise_var, "factors": factors, "gains": gains, "solution": solution, "residual": residual, "direction": direction}


def leaf_apply(blocks):
    scaled_leaf, sq_leaf, dir_leaf, signal = blocks
    inner = jnp.dot(scaled_leaf.T, scaled_leaf, precision=lax.Precision.HIGHEST, preferred_element_type=jnp.float32)
    kernel = signal * jnp.exp(-0.5 * (sq_leaf[:, None] + sq_leaf[None, :] - 2.0 * inner))
    return jnp.dot(dir_leaf, kernel.T, precision=lax.Precision.HIGHEST, preferred_element_type=jnp.float32)


def reference(features, lengthscale, signal_var, noise_var, factors, gains, solution, residual, direction):
    scaled = features.astype(jnp.float32) / lengthscale[:, None]
    sq_norm = jnp.sum(scaled * scaled, axis=0)
    leaves = POINTS // LEAF
    scaled_leaves = scaled.reshape(F, leaves, LEAF).transpose(1, 0, 2)
    sq_leaves = sq_norm.reshape(leaves, LEAF)
    dir_leaves = direction.reshape(C, leaves, LEAF).transpose(1, 0, 2)
    signal = jnp.broadcast_to(signal_var[0], (leaves,))
    leaf_term = lax.map(leaf_apply, (scaled_leaves, sq_leaves, dir_leaves, signal))
    image = noise_var[0] * direction + leaf_term.transpose(1, 0, 2).reshape(C, POINTS)
    direction_low = direction.astype(jnp.bfloat16)
    for level in range(1, LEVELS + 1):
        child = LEAF * 2 ** (level - 1)
        nodes = POINTS // (2 * child)
        basis = factors[level - 1].reshape(nodes, 2, child, R).astype(jnp.float32)
        pieces = direction_low.reshape(C, nodes, 2, child).astype(jnp.float32)
        projection = jnp.einsum("cnsm,nsmr->nscr", pieces, basis, precision=lax.Precision.HIGHEST)
        sibling = projection[:, ::-1]
        weighted = (gains[level - 1][None, None, None, :] * sibling).astype(jnp.bfloat16)
        spread = jnp.einsum("nscr,nsmr->cnsm", weighted.astype(jnp.float32), basis, precision=lax.Precision.HIGHEST)
        image = image + spread.reshape(C, POINTS)
    norm_now = jnp.sum(residual * residual, axis=1)
    curvature = jnp.sum(direction * image, axis=1)
    step_size = norm_now / curvature
    new_solution = solution + step_size[:, None] * direction
    new_residual = residual - step_size[:, None] * image
    norm_next = jnp.sum(new_residual * new_residual, axis=1)
    new_direction = new_residual + (norm_next / norm_now)[:, None] * direction
    return new_solution, new_residual, new_direction
```

```python
import jax
import jax.numpy as jnp
import numpy as np
from jax import lax
from jax.experimental import pallas as pl
from jax.experimental.pallas import tpu as pltpu
from jax.sharding import Mesh, PartitionSpec as P

LOG2E = 1.4426950408889634
CHIP = ("x", "y")
LEAF = ("x", "y", "core")
BF = jnp.bfloat16
F32 = jnp.float32


def parts_of(value, count):
    parts = []
    for _ in range(count):
        part = value.astype(BF)
        parts.append(part)
        value = value - part.astype(F32)
    return parts


def leaf_kernel(signal_ref, rate_ref, own_ref, other_ref, out_ref):
    points = own_ref.shape[1]
    rate = rate_ref[...]
    row = lax.broadcasted_iota(jnp.int32, (16, points), 0)
    ones = jnp.where(row < 3, 1.0, 0.0).astype(BF)

    def prepared(ref):
        feat = ref[0:64, :]
        wide = feat.astype(F32)
        scaled = wide * rate
        half = -0.5 * jnp.sum(wide * scaled, axis=0, keepdims=True)
        one, two, three = [part.astype(F32) for part in parts_of(half, 3)]
        halves = jnp.where(row == 0, one, jnp.where(row == 1, two, jnp.where(row == 2, three, 0.0)))
        return feat, scaled, halves.astype(BF)

    feat, scaled, halves = prepared(own_ref)
    other_feat, _, other_halves = prepared(other_ref)
    left = jnp.concatenate(parts_of(scaled, 3) + [halves, ones], axis=0).T
    right = [
        jnp.concatenate([feat, feat, feat, ones, halves], axis=0),
        jnp.concatenate([other_feat, other_feat, other_feat, ones, other_halves], axis=0),
    ]
    values = [own_ref[64:192, :], other_ref[64:192, :]]
    tile = 256
    for start in range(0, points, tile):
        both = jnp.zeros((tile, 128), F32)
        low = jnp.zeros((tile, 64), F32)
        for side in range(2):
            power = jnp.dot(left[start : start + tile], right[side], preferred_element_type=F32)
            kernel = jnp.exp2(power)
            high_part, low_part = parts_of(kernel, 2)
            dims = (((1,), (1,)), ((), ()))
            both += lax.dot_general(high_part, values[side], dims, preferred_element_type=F32)
            low += lax.dot_general(low_part, values[side][0:64], dims, preferred_element_type=F32)
        turned = both.T
        out_ref[:, start : start + tile] = signal_ref[0] * (turned[0:64] + turned[64:128] + low.T)


def leaf_term(signal, rate, own, other):
    return pl.pallas_call(
        leaf_kernel,
        out_shape=jax.ShapeDtypeStruct((64, own.shape[1]), F32),
        in_specs=[pl.BlockSpec(memory_space=pltpu.SMEM)] + [pl.BlockSpec(memory_space=pltpu.VMEM)] * 3,
        out_specs=pl.BlockSpec(memory_space=pltpu.VMEM),
        compiler_params=pltpu.CompilerParams(vmem_limit_bytes=40 * 1024 * 1024),
        cost_estimate=pl.CostEstimate(
            flops=2 * 1024 * 2048 * 256 * 3, bytes_accessed=2**20, transcendentals=1024 * 2048
        ),
    )(signal, rate, own, other)


def level_mask(count, mine):
    other = jnp.arange(count, dtype=jnp.int32)[:, None]
    low = jnp.left_shift(1, jnp.arange(4, dtype=jnp.int32))[None, :]
    apart = jnp.bitwise_xor(other, mine)
    return ((apart >= low) & (apart < 2 * low)).astype(BF)


def local(
    features, lengthscale, signal_var, noise_var, factors, gains, solution, residual, direction
):
    core = lax.axis_index("core")
    chip = lax.axis_index(CHIP)
    plane = lax.axis_index("z")

    direction_low, direction_rest = parts_of(direction, 2)
    own = jnp.concatenate([features, direction_low, direction_rest], axis=0)
    other = lax.ppermute(own, "core", [(0, 1), (1, 0)])

    projection = jnp.einsum(
        "cp,lpr->lcr", direction_low, factors, preferred_element_type=F32
    ).astype(BF)
    near = level_mask(16, chip)
    far = level_mask(16, plane)
    near_out = jnp.einsum("jk,khcr->jhcr", near, projection[:4].reshape(4, 2, 32, 128))
    far_out = projection[4:].reshape(4, 2, 32, 128).transpose(2, 0, 1, 3)
    sent = jnp.concatenate([near_out.reshape(32, 32, 128), far_out.reshape(32, 8, 128)], axis=1)
    got = lax.all_to_all(sent, LEAF, 0, 0, tiled=True)

    rate = (LOG2E / (lengthscale * lengthscale))[:, None]
    image = noise_var[0] * direction + leaf_term(signal_var, rate, own, other)

    plane_sum = jnp.sum(got[:, 32:].astype(F32), axis=0).astype(BF).reshape(4, 2, 128)
    far_sent = jnp.einsum("jk,kcr->jcr", far, plane_sum)
    far_got = lax.all_to_all(far_sent, "z", 0, 0, tiled=True)

    near_sum = jnp.einsum(
        "jk,jhcr->kcr", near, got[:, :32].reshape(16, 2, 32, 128), preferred_element_type=F32
    )
    near_weighted = (gains[:4, None, :] * near_sum).astype(BF)
    near_other = lax.ppermute(near_weighted, "core", [(0, 1), (1, 0)])
    near_all = jnp.where(
        core == 0,
        jnp.concatenate([near_weighted, near_other], axis=1),
        jnp.concatenate([near_other, near_weighted], axis=1),
    )

    far_sum = jnp.einsum("jk,jcr->kcr", far, far_got, preferred_element_type=F32)
    far_weighted = (gains[4:, None, :] * far_sum).astype(BF)
    far_all = lax.all_to_all(
        jnp.broadcast_to(far_weighted[None], (32, 4, 2, 128)), LEAF, 0, 0, tiled=True
    )
    far_all = far_all.transpose(1, 2, 0, 3).reshape(4, 64, 128)
    weighted = jnp.concatenate([near_all, far_all], axis=0)

    image = image + jnp.einsum("lcr,lpr->cp", weighted, factors, preferred_element_type=F32)

    def total(stats):
        stats = lax.all_to_all(
            jnp.broadcast_to(stats[None], (16,) + stats.shape), CHIP, 0, 0, tiled=True
        ).sum(0)
        return lax.all_to_all(
            jnp.broadcast_to(stats[None], (32,) + stats.shape), ("core", "z"), 0, 0, tiled=True
        ).sum(0)

    stats = jnp.stack(
        [
            jnp.sum(residual * residual, axis=1),
            jnp.sum(direction * image, axis=1),
            jnp.sum(residual * image, axis=1),
            jnp.sum(image * image, axis=1),
        ]
    )
    norm_now, curvature, cross, square = total(stats.reshape(1, 256)).reshape(4, 64)
    step_size = norm_now / curvature
    norm_next = jnp.maximum(norm_now + step_size * (step_size * square - 2.0 * cross), 0.0)
    new_solution = solution + step_size[:, None] * direction
    new_residual = residual - step_size[:, None] * image
    new_direction = new_residual + (norm_next / norm_now)[:, None] * direction
    return (new_solution, new_residual, new_direction)


def solution(mesh):
    fine = Mesh(mesh.devices.reshape(4, 4, 2, 16), ("x", "y", "core", "z"))
    points = P(None, ("z", "x", "y", "core"))
    return jax.shard_map(
        local,
        mesh=fine,
        in_specs=(
            points,
            P(),
            P(),
            P(),
            P(None, ("z", "x", "y", "core"), None),
            P(),
            points,
            points,
            points,
        ),
        out_specs=(points, points, points),
        check_vma=False,
    )
```

```python
import jax
import jax.numpy as jnp
import numpy as np
from jax import lax
from jax.experimental import pallas as pl
from jax.experimental.pallas import tpu as pltpu
from jax.sharding import Mesh, PartitionSpec as P

LOG2E = 1.4426950408889634
CHIP = ("x", "y")
LEAF = ("x", "y", "core")
ROW = ("y", "core")
VMEM = pl.BlockSpec(memory_space=pltpu.VMEM)
SMEM = pl.BlockSpec(memory_space=pltpu.SMEM)
HBM = pl.BlockSpec(memory_space=pltpu.HBM)
SWAP = [(0, 1), (1, 0)]
BF = jnp.bfloat16
F32 = jnp.float32


def parts_of(value, count):
    parts = []
    for _ in range(count):
        part = value.astype(BF)
        parts.append(part)
        value = value - part.astype(F32)
    return parts


def leaf_kernel(signal_ref, rate_ref, own_ref, other_ref, *refs):
    out_ref = refs[-1]
    points = own_ref.shape[1]
    rate = rate_ref[...]
    row = lax.broadcasted_iota(jnp.int32, (16, points), 0)
    ones = jnp.where(row < 3, 1.0, 0.0).astype(BF)

    def prepared(ref):
        feat = ref[0:64, :]
        wide = feat.astype(F32)
        scaled = wide * rate
        half = -0.5 * jnp.sum(wide * scaled, axis=0, keepdims=True)
        one, two, three = [part.astype(F32) for part in parts_of(half, 3)]
        halves = jnp.where(row == 0, one, jnp.where(row == 1, two, jnp.where(row == 2, three, 0.0)))
        return feat, scaled, halves.astype(BF)

    _, scaled, halves = prepared(own_ref)
    feat, _, other_halves = prepared(other_ref)
    left = jnp.concatenate(parts_of(scaled, 3) + [halves, ones], axis=0).T
    right = jnp.concatenate([feat, feat, feat, ones, other_halves], axis=0)
    value = other_ref[64:192, :]
    dims = (((1,), (1,)), ((), ()))
    tile = 256
    for start in range(0, points, tile):
        here = slice(start, start + tile)
        power = jnp.dot(left[here], right, preferred_element_type=F32)
        high, low = parts_of(jnp.exp2(power), 2)
        both = lax.dot_general(high, value, dims, preferred_element_type=F32).T
        rest = lax.dot_general(low, value[0:64], dims, preferred_element_type=F32).T
        result = signal_ref[0] * (both[0:64] + both[64:128] + rest)
        if len(refs) > 1:
            result += refs[0][:, here]
        out_ref[:, here] = result


def leaf_term(signal, rate, own, other, *base):
    return pl.pallas_call(
        leaf_kernel,
        out_shape=jax.ShapeDtypeStruct((64, own.shape[1]), F32),
        in_specs=[SMEM] + [VMEM] * (3 + len(base)),
        out_specs=VMEM,
        compiler_params=pltpu.CompilerParams(vmem_limit_bytes=40 * 2**20),
        cost_estimate=pl.CostEstimate(
            flops=2 * 1024 * 1024 * 256 * 3, bytes_accessed=2**20, transcendentals=1024 * 1024
        ),
    )(signal, rate, own, other, *base)


def image_kernel(
    place_ref,
    noise_ref,
    near_ref,
    near_other_ref,
    far_ref,
    factors_ref,
    leaf_ref,
    direction_ref,
    residual_ref,
    image_ref,
    stats_ref,
):
    first = place_ref[0] == 0
    levels = []
    for k in range(4):
        own, other = near_ref[k].astype(F32), near_other_ref[k].astype(F32)
        low = jnp.where(first, own, other)
        high = jnp.where(first, other, own)
        levels.append(jnp.concatenate([low, high], axis=0).astype(BF))
    levels += [far_ref[k] for k in range(4)]
    pairs = [jnp.concatenate(levels[k : k + 2], axis=1) for k in range(0, 8, 2)]
    points = direction_ref.shape[1]
    tile = 256
    sums = [jnp.zeros((64, 128), F32) for _ in range(4)]
    for start in range(0, points, tile):
        here = slice(start, start + tile)
        direction, residual = direction_ref[:, here], residual_ref[:, here]
        image = noise_ref[0] * direction + leaf_ref[:, here]
        for k in range(0, 8, 2):
            basis = jnp.concatenate([factors_ref[k, here, :], factors_ref[k + 1, here, :]], axis=1)
            image += lax.dot_general(
                pairs[k // 2], basis, (((1,), (1,)), ((), ())), preferred_element_type=F32
            )
        image_ref[:, here] = image
        products = [residual * residual, direction * image, residual * image, image * image]
        for n, product in enumerate(products):
            for lane in range(0, tile, 128):
                sums[n] += product[:, lane : lane + 128]
    row = jnp.sum(jnp.concatenate(sums, axis=0).T, axis=0, keepdims=True)
    for to in range(16):
        stats_ref[to] = row


def step_kernel(
    stats_ref, solution_ref, residual_ref, direction_ref, image_ref, out0, out1, out2, held, sems
):
    stats = stats_ref[0]
    for source in range(1, 32):
        stats += stats_ref[source]
    norm_now, curvature, cross, square = [stats[:, 64 * n : 64 * n + 64] for n in range(4)]
    step_size = norm_now / curvature
    norm_next = jnp.maximum(norm_now + step_size * (step_size * square - 2.0 * cross), 0.0)
    ratio = norm_next / norm_now
    rows = jnp.concatenate([step_size, ratio], axis=1)
    columns = jnp.broadcast_to(rows, (128, 128)).T
    step_size, ratio = columns[0:64, 0:1], columns[64:128, 0:1]
    outs = (out0, out1, out2)
    copies = []
    for part in range(4):
        here = pl.ds(16 * part, 16)
        step, beta = step_size[16 * part : 16 * part + 16], ratio[16 * part : 16 * part + 16]
        direction = direction_ref[here, :]
        new_residual = residual_ref[here, :] - step * image_ref[here, :]
        held[0, here, :] = solution_ref[here, :] + step * direction
        held[1, here, :] = new_residual
        held[2, here, :] = new_residual + beta * direction
        for n in range(3):
            copy = pltpu.make_async_copy(
                held.at[n, here, :], outs[n].at[here, :], sems.at[3 * part + n]
            )
            copy.start()
            copies.append(copy)
    for copy in copies:
        copy.wait()


def call(kernel, outs, specs, *operands, scratch=(), flops=0, out_spec=VMEM):
    shapes = [jax.ShapeDtypeStruct(shape, dtype) for shape, dtype in outs]
    size = sum(o.size * o.dtype.itemsize for o in operands)
    size += sum(s.size * s.dtype.itemsize for s in shapes)
    single = len(shapes) == 1
    return pl.pallas_call(
        kernel,
        out_shape=shapes[0] if single else shapes,
        in_specs=specs,
        out_specs=out_spec if single else [out_spec] * len(shapes),
        scratch_shapes=list(scratch),
        compiler_params=pltpu.CompilerParams(vmem_limit_bytes=32 * 2**20),
        cost_estimate=pl.CostEstimate(flops=flops, bytes_accessed=size, transcendentals=0),
    )(*operands)


def meets(mine):
    apart = jnp.bitwise_xor(jnp.arange(16, dtype=jnp.int32)[:, None], mine)
    low = jnp.left_shift(1, jnp.arange(4, dtype=jnp.int32))[None, :]
    return (apart >= low) & (apart < 2 * low)


def local(
    features, lengthscale, signal_var, noise_var, factors, gains, solution, residual, direction
):
    core = lax.axis_index("core")
    place = core.astype(jnp.int32).reshape(1)

    projection = jnp.einsum(
        "cp,lpr->lcr", direction.astype(BF), factors, preferred_element_type=F32
    ).astype(BF)
    near_meets = meets(lax.axis_index(CHIP)).reshape(16, 1, 4, 1, 1)
    far_meets = meets(lax.axis_index("z")).reshape(16, 4, 1, 1)
    near = projection[:4].reshape(4, 2, 32, 128).transpose(1, 0, 2, 3)[None]
    near = jnp.sum(jnp.where(near_meets, near, 0.0).astype(F32), axis=2).astype(BF)
    far = projection[4:].reshape(4, 2, 32, 128).transpose(2, 0, 1, 3)
    sent = jnp.concatenate([near.reshape(32, 32, 128), far.reshape(32, 8, 128)], axis=1)
    got = lax.all_to_all(sent, LEAF, 0, 0, tiled=True)

    own = jnp.concatenate([features] + parts_of(lax.optimization_barrier(direction), 2), axis=0)
    other = lax.ppermute(own, "core", SWAP)
    rate = (LOG2E / (lengthscale * lengthscale))[:, None]
    leaf = leaf_term(signal_var, rate, own, own)
    got, leaf = lax.optimization_barrier((got, leaf))
    leaf = leaf_term(signal_var, rate, own, other, leaf)

    plane_sum = jnp.sum(got[:, 32:].astype(F32), axis=0).reshape(1, 4, 2, 128)
    far = jnp.sum(jnp.where(far_meets, plane_sum, 0.0), axis=1).astype(BF)
    far = lax.all_to_all(far, "z", 0, 0, tiled=True)

    near = jnp.sum(got[:, :32].astype(F32).reshape(16, 2, 1, 32, 128), axis=1)
    near = jnp.sum(jnp.where(near_meets.reshape(16, 4, 1, 1), near, 0.0), axis=0)
    near = (gains[:4, None, :] * near).astype(BF)
    near_other = lax.ppermute(near, "core", SWAP)

    far = jnp.sum(jnp.where(far_meets, far.astype(F32)[:, None], 0.0), axis=0)
    far = (gains[4:, None, :] * far).astype(BF).reshape(1, 8, 128)
    far = lax.all_to_all(jnp.broadcast_to(far, (32, 8, 128)), LEAF, 0, 0, tiled=True)
    far = far.reshape(32, 4, 2, 128).transpose(1, 2, 0, 3).reshape(4, 64, 128)

    image, stats = call(
        image_kernel, [((64, 1024), F32), ((16, 1, 256), F32)],
        [SMEM, SMEM] + [VMEM] * 7,
        place, noise_var, near, near_other, far, factors, leaf, direction, residual, flops=2**27,
    )
    stats = lax.all_to_all(stats, CHIP, 0, 0, tiled=True).sum(0)
    stats = jnp.broadcast_to(stats[None], (32, 1, 256))
    stats = lax.all_to_all(stats, ("core", "z"), 0, 0, tiled=True)
    return call(
        step_kernel, [(direction.shape, F32)] * 3, [VMEM] * 5,
        stats, solution, residual, direction, image,
        scratch=[pltpu.VMEM((3,) + direction.shape, F32), pltpu.SemaphoreType.DMA((12,))],
        out_spec=HBM,
    )


def solution(mesh):
    fine = Mesh(mesh.devices.reshape(4, 4, 2, 16), ("x", "y", "core", "z"))
    points = P(None, ("z", "x", "y", "core"))
    return jax.shard_map(
        local,
        mesh=fine,
        in_specs=(
            points,
            P(),
            P(),
            P(),
            P(None, ("z", "x", "y", "core"), None),
            P(),
            points,
            points,
            points,
        ),
        out_specs=(points, points, points),
        check_vma=False,
    )
```

```python
import jax
import jax.numpy as jnp
import numpy as np
from jax import lax
from jax.experimental import pallas as pl
from jax.experimental.pallas import tpu as pltpu
from jax.sharding import Mesh, PartitionSpec as P

LOG2E = 1.4426950408889634
CHIP = ("x", "y")
LEAF = ("x", "y", "core")
ROW = ("y", "core")
VMEM = pl.BlockSpec(memory_space=pltpu.VMEM)
SMEM = pl.BlockSpec(memory_space=pltpu.SMEM)
HBM = pl.BlockSpec(memory_space=pltpu.HBM)
SWAP = [(0, 1), (1, 0)]
PLANES = [8, 0, 15, 1, 14, 2, 13, 3, 12, 4, 11, 5, 10, 6, 9, 7]
COLUMN = [24, 16, 31, 17, 30, 18, 29, 19, 28, 20, 27, 21, 26, 22, 25, 23, 8, 0, 15, 1, 14, 2, 13, 3, 12, 4, 11, 5, 10, 6, 9, 7]
CHIPS = [15, 14, 13, 12, 11, 10, 9, 8, 7, 6, 5, 4, 3, 2, 1, 0]
LEAVES = [30, 31, 28, 29, 26, 27, 24, 25, 22, 23, 20, 21, 18, 19, 16, 17, 14, 15, 12, 13, 10, 11, 8, 9, 6, 7, 4, 5, 2, 3, 0, 1]
SQUARE = [15, 14, 13, 12, 11, 10, 9, 8, 7, 6, 5, 4, 3, 2, 1, 0]
BF = jnp.bfloat16
F32 = jnp.float32


def parts_of(value, count):
    parts = []
    for _ in range(count):
        part = value.astype(BF)
        parts.append(part)
        value = value - part.astype(F32)
    return parts


def leaf_kernel(signal_ref, rate_ref, own_ref, other_ref, *refs):
    out_ref = refs[-1]
    points = own_ref.shape[1]
    rate = rate_ref[...]
    row = lax.broadcasted_iota(jnp.int32, (16, points), 0)
    ones = jnp.where(row < 3, 1.0, 0.0).astype(BF)

    def prepared(ref):
        feat = ref[0:64, :]
        wide = feat.astype(F32)
        scaled = wide * rate
        half = -0.5 * jnp.sum(wide * scaled, axis=0, keepdims=True)
        one, two, three = [part.astype(F32) for part in parts_of(half, 3)]
        halves = jnp.where(row == 0, one, jnp.where(row == 1, two, jnp.where(row == 2, three, 0.0)))
        return feat, scaled, halves.astype(BF)

    _, scaled, halves = prepared(own_ref)
    feat, _, other_halves = prepared(other_ref)
    left = jnp.concatenate(parts_of(scaled, 3) + [halves, ones], axis=0).T
    right = jnp.concatenate([feat, feat, feat, ones, other_halves], axis=0)
    value = other_ref[64:192, :]
    dims = (((1,), (1,)), ((), ()))
    tile = 256
    for start in range(0, points, tile):
        here = slice(start, start + tile)
        power = jnp.dot(left[here], right, preferred_element_type=F32)
        high, low = parts_of(jnp.exp2(power), 2)
        both = lax.dot_general(high, value, dims, preferred_element_type=F32).T
        rest = lax.dot_general(low, value[0:64], dims, preferred_element_type=F32).T
        result = signal_ref[0] * (both[0:64] + both[64:128] + rest)
        if len(refs) > 1:
            result += refs[0][:, here]
        out_ref[:, here] = result


def leaf_term(signal, rate, own, other, *base):
    return pl.pallas_call(
        leaf_kernel,
        out_shape=jax.ShapeDtypeStruct((64, own.shape[1]), F32),
        in_specs=[SMEM] + [VMEM] * (3 + len(base)),
        out_specs=VMEM,
        compiler_params=pltpu.CompilerParams(vmem_limit_bytes=40 * 2**20),
        cost_estimate=pl.CostEstimate(
            flops=2 * 1024 * 1024 * 256 * 3, bytes_accessed=2**20, transcendentals=1024 * 1024
        ),
    )(signal, rate, own, other, *base)


def image_kernel(
    place_ref,
    noise_ref,
    near_ref,
    near_other_ref,
    far_ref,
    factors_ref,
    leaf_ref,
    direction_ref,
    residual_ref,
    image_ref,
    stats_ref,
):
    first = place_ref[0] == 0
    levels = []
    for k in range(4):
        own, other = near_ref[k].astype(F32), near_other_ref[k].astype(F32)
        low = jnp.where(first, own, other)
        high = jnp.where(first, other, own)
        levels.append(jnp.concatenate([low, high], axis=0).astype(BF))
    levels += [far_ref[k] for k in range(4)]
    pairs = [jnp.concatenate(levels[k : k + 2], axis=1) for k in range(0, 8, 2)]
    points = direction_ref.shape[1]
    tile = 256
    sums = [jnp.zeros((64, 128), F32) for _ in range(4)]
    for start in range(0, points, tile):
        here = slice(start, start + tile)
        direction, residual = direction_ref[:, here], residual_ref[:, here]
        image = noise_ref[0] * direction + leaf_ref[:, here]
        for k in range(0, 8, 2):
            basis = jnp.concatenate([factors_ref[k, here, :], factors_ref[k + 1, here, :]], axis=1)
            image += lax.dot_general(
                pairs[k // 2], basis, (((1,), (1,)), ((), ())), preferred_element_type=F32
            )
        image_ref[:, here] = image
        products = [residual * residual, direction * image, residual * image, image * image]
        for n, product in enumerate(products):
            for lane in range(0, tile, 128):
                sums[n] += product[:, lane : lane + 128]
    row = jnp.sum(jnp.concatenate(sums, axis=0).T, axis=0, keepdims=True)
    for to in range(16):
        stats_ref[to] = row


def step_kernel(
    stats_ref, solution_ref, residual_ref, direction_ref, image_ref, out0, out1, out2, held, sems
):
    stats = stats_ref[0]
    for source in range(1, 32):
        stats += stats_ref[source]
    norm_now, curvature, cross, square = [stats[:, 64 * n : 64 * n + 64] for n in range(4)]
    step_size = norm_now / curvature
    norm_next = jnp.maximum(norm_now + step_size * (step_size * square - 2.0 * cross), 0.0)
    ratio = norm_next / norm_now
    rows = jnp.concatenate([step_size, ratio], axis=1)
    columns = jnp.broadcast_to(rows, (128, 128)).T
    step_size, ratio = columns[0:64, 0:1], columns[64:128, 0:1]
    outs = (out0, out1, out2)
    copies = []
    for part in range(4):
        here = pl.ds(16 * part, 16)
        step, beta = step_size[16 * part : 16 * part + 16], ratio[16 * part : 16 * part + 16]
        direction = direction_ref[here, :]
        new_residual = residual_ref[here, :] - step * image_ref[here, :]
        held[0, here, :] = solution_ref[here, :] + step * direction
        held[1, here, :] = new_residual
        held[2, here, :] = new_residual + beta * direction
        for n in range(3):
            copy = pltpu.make_async_copy(
                held.at[n, here, :], outs[n].at[here, :], sems.at[3 * part + n]
            )
            copy.start()
            copies.append(copy)
    for copy in copies:
        copy.wait()


def call(kernel, outs, specs, *operands, scratch=(), flops=0, out_spec=VMEM):
    shapes = [jax.ShapeDtypeStruct(shape, dtype) for shape, dtype in outs]
    size = sum(o.size * o.dtype.itemsize for o in operands)
    size += sum(s.size * s.dtype.itemsize for s in shapes)
    single = len(shapes) == 1
    return pl.pallas_call(
        kernel,
        out_shape=shapes[0] if single else shapes,
        in_specs=specs,
        out_specs=out_spec if single else [out_spec] * len(shapes),
        scratch_shapes=list(scratch),
        compiler_params=pltpu.CompilerParams(vmem_limit_bytes=32 * 2**20),
        cost_estimate=pl.CostEstimate(flops=flops, bytes_accessed=size, transcendentals=0),
    )(*operands)


def meets(mine, order):
    apart = jnp.bitwise_xor(jnp.array(order, dtype=jnp.int32)[:, None], mine)
    low = jnp.left_shift(1, jnp.arange(4, dtype=jnp.int32))[None, :]
    return (apart >= low) & (apart < 2 * low)


def local(
    features, lengthscale, signal_var, noise_var, factors, gains, solution, residual, direction
):
    core = lax.axis_index("core")
    place = core.astype(jnp.int32).reshape(1)

    projection = jnp.einsum(
        "cp,lpr->lcr", direction.astype(BF), factors, preferred_element_type=F32
    ).astype(BF)
    near_meets = meets(lax.axis_index(CHIP), CHIPS).reshape(16, 1, 4, 1, 1)
    far_meets = meets(lax.axis_index("z"), PLANES).reshape(16, 4, 1, 1)
    near = projection[:4].reshape(4, 2, 32, 128).transpose(1, 0, 2, 3)[None]
    near = jnp.sum(jnp.where(near_meets, near, 0.0).astype(F32), axis=2).astype(BF)
    far = projection[4:].reshape(4, 2, 32, 128).transpose(2, 0, 1, 3)
    sent = jnp.concatenate([near.reshape(32, 32, 128), far.reshape(32, 8, 128)], axis=1)
    got = lax.all_to_all(sent, LEAF, 0, 0, tiled=True, axis_index_groups=[LEAVES])

    own = jnp.concatenate([features] + parts_of(lax.optimization_barrier(direction), 2), axis=0)
    other = lax.ppermute(own, "core", SWAP)
    rate = (LOG2E / (lengthscale * lengthscale))[:, None]
    leaf = leaf_term(signal_var, rate, own, own)
    got, leaf = lax.optimization_barrier((got, leaf))
    leaf = leaf_term(signal_var, rate, own, other, leaf)

    plane_sum = jnp.sum(got[:, 32:].astype(F32), axis=0).reshape(1, 4, 2, 128)
    far = jnp.sum(jnp.where(far_meets, plane_sum, 0.0), axis=1).astype(BF)
    far = lax.all_to_all(far, "z", 0, 0, tiled=True, axis_index_groups=[PLANES])

    near = jnp.sum(got[:, :32].astype(F32).reshape(16, 2, 1, 32, 128), axis=1)
    near = jnp.sum(jnp.where(near_meets.reshape(16, 4, 1, 1), near, 0.0), axis=0)
    near = (gains[:4, None, :] * near).astype(BF)
    near_other = lax.ppermute(near, "core", SWAP)

    far = jnp.sum(jnp.where(far_meets, far.astype(F32)[:, None], 0.0), axis=0)
    far = (gains[4:, None, :] * far).astype(BF).reshape(1, 8, 128)
    far = lax.all_to_all(jnp.broadcast_to(far, (32, 8, 128)), LEAF, 0, 0, tiled=True, axis_index_groups=[LEAVES])
    far = far.reshape(32, 4, 2, 128).transpose(1, 2, 0, 3).reshape(4, 64, 128)

    image, stats = call(
        image_kernel, [((64, 1024), F32), ((16, 1, 256), F32)],
        [SMEM, SMEM] + [VMEM] * 7,
        place, noise_var, near, near_other, far, factors, leaf, direction, residual, flops=2**27,
    )
    stats = lax.all_to_all(stats, CHIP, 0, 0, tiled=True, axis_index_groups=[SQUARE]).sum(0)
    stats = jnp.broadcast_to(stats[None], (32, 1, 256))
    stats = lax.all_to_all(stats, ("core", "z"), 0, 0, tiled=True, axis_index_groups=[COLUMN])
    return call(
        step_kernel, [(direction.shape, F32)] * 3, [VMEM] * 5,
        stats, solution, residual, direction, image,
        scratch=[pltpu.VMEM((3,) + direction.shape, F32), pltpu.SemaphoreType.DMA((12,))],
        out_spec=HBM,
    )


def solution(mesh):
    fine = Mesh(mesh.devices.reshape(4, 4, 2, 16), ("x", "y", "core", "z"))
    points = P(None, ("z", "x", "y", "core"))
    return jax.shard_map(
        local,
        mesh=fine,
        in_specs=(
            points,
            P(),
            P(),
            P(),
            P(None, ("z", "x", "y", "core"), None),
            P(),
            points,
            points,
            points,
        ),
        out_specs=(points, points, points),
        check_vma=False,
    )
```

```python
import jax
import jax.numpy as jnp
import numpy as np
from jax import lax
from jax.experimental import pallas as pl
from jax.experimental.pallas import tpu as pltpu
from jax.sharding import Mesh, PartitionSpec as P

LOG2E = 1.4426950408889634
CHIP = ("x", "y")
LEAF = ("x", "y", "core")
ROW = ("y", "core")
VMEM = pl.BlockSpec(memory_space=pltpu.VMEM)
SMEM = pl.BlockSpec(memory_space=pltpu.SMEM)
HBM = pl.BlockSpec(memory_space=pltpu.HBM)
SWAP = [(0, 1), (1, 0)]
PLANES = [z ^ 8 for z in range(16)]
COLUMN = [16 * core + z for core in (1, 0) for z in PLANES]
LEAVES = [leaf ^ 30 for leaf in range(32)]
SQUARE = [chip ^ 15 for chip in range(16)]
BF = jnp.bfloat16
F32 = jnp.float32


def parts_of(value, count):
    parts = []
    for _ in range(count):
        part = value.astype(BF)
        parts.append(part)
        value = value - part.astype(F32)
    return parts


def leaf_kernel(signal_ref, rate_ref, own_ref, other_ref, *refs):
    out_ref = refs[-1]
    points = own_ref.shape[1]
    rate = rate_ref[...]
    row = lax.broadcasted_iota(jnp.int32, (16, points), 0)
    ones = jnp.where(row < 3, 1.0, 0.0).astype(BF)

    def prepared(ref):
        feat = ref[0:64, :]
        wide = feat.astype(F32)
        scaled = wide * rate
        half = -0.5 * jnp.sum(wide * scaled, axis=0, keepdims=True)
        one, two, three = [part.astype(F32) for part in parts_of(half, 3)]
        halves = jnp.where(row == 0, one, jnp.where(row == 1, two, jnp.where(row == 2, three, 0.0)))
        return feat, scaled, halves.astype(BF)

    _, scaled, halves = prepared(own_ref)
    feat, _, other_halves = prepared(other_ref)
    left = jnp.concatenate(parts_of(scaled, 3) + [halves, ones], axis=0).T
    right = jnp.concatenate([feat, feat, feat, ones, other_halves], axis=0)
    value = other_ref[64:192, :]
    dims = (((1,), (1,)), ((), ()))
    tile = 256
    for start in range(0, points, tile):
        here = slice(start, start + tile)
        power = jnp.dot(left[here], right, preferred_element_type=F32)
        high, low = parts_of(jnp.exp2(power), 2)
        both = lax.dot_general(high, value, dims, preferred_element_type=F32).T
        rest = lax.dot_general(low, value[0:64], dims, preferred_element_type=F32).T
        result = signal_ref[...] * (both[0:64] + both[64:128] + rest)
        if len(refs) > 1:
            result += refs[0][:, here]
        out_ref[:, here] = result


def leaf_term(signal, rate, own, other, *base):
    return pl.pallas_call(
        leaf_kernel,
        out_shape=jax.ShapeDtypeStruct((64, own.shape[1]), F32),
        in_specs=[VMEM] * (4 + len(base)),
        out_specs=VMEM,
        compiler_params=pltpu.CompilerParams(vmem_limit_bytes=40 * 2**20),
        cost_estimate=pl.CostEstimate(
            flops=2 * 1024 * 1024 * 256 * 3, bytes_accessed=2**20, transcendentals=1024 * 1024
        ),
    )(signal, rate, own, other, *base)


def spread(levels, factors_ref, here):
    total = None
    for k in range(0, 4, 2):
        pair = jnp.concatenate(levels[k : k + 2], axis=1)
        basis = jnp.concatenate([factors_ref[k, here, :], factors_ref[k + 1, here, :]], axis=1)
        part = lax.dot_general(
            pair, basis, (((1,), (1,)), ((), ())), preferred_element_type=F32
        )
        total = part if total is None else total + part
    return total


def near_kernel(
    place_ref, noise_ref, near_ref, near_other_ref, factors_ref, leaf_ref, direction_ref, out_ref
):
    first = place_ref[0] == 0
    levels = []
    for k in range(4):
        own, other = near_ref[k].astype(F32), near_other_ref[k].astype(F32)
        low = jnp.where(first, own, other)
        high = jnp.where(first, other, own)
        levels.append(jnp.concatenate([low, high], axis=0).astype(BF))
    for start in range(0, direction_ref.shape[1], 256):
        here = slice(start, start + 256)
        base = noise_ref[...] * direction_ref[:, here] + leaf_ref[:, here]
        out_ref[:, here] = base + spread(levels, factors_ref, here)


def image_kernel(
    far_ref, factors_ref, base_ref, direction_ref, residual_ref, image_ref, stats_ref
):
    levels = [far_ref[k] for k in range(4)]
    tile = 256
    sums = [jnp.zeros((64, 128), F32) for _ in range(4)]
    for start in range(0, direction_ref.shape[1], tile):
        here = slice(start, start + tile)
        direction, residual = direction_ref[:, here], residual_ref[:, here]
        image = base_ref[:, here] + spread(levels, factors_ref.at[4:8], here)
        image_ref[:, here] = image
        products = [residual * residual, direction * image, residual * image, image * image]
        for n, product in enumerate(products):
            for lane in range(0, tile, 128):
                sums[n] += product[:, lane : lane + 128]
    row = jnp.sum(jnp.concatenate(sums, axis=0).T, axis=0, keepdims=True)
    for to in range(16):
        stats_ref[to] = row


def step_kernel(
    stats_ref, solution_ref, residual_ref, direction_ref, image_ref, out0, out1, out2, held, sems
):
    stats = stats_ref[0]
    for source in range(1, 32):
        stats += stats_ref[source]
    norm_now, curvature, cross, square = [stats[:, 64 * n : 64 * n + 64] for n in range(4)]
    step_size = norm_now / curvature
    norm_next = jnp.maximum(norm_now + step_size * (step_size * square - 2.0 * cross), 0.0)
    ratio = norm_next / norm_now
    rows = jnp.concatenate([step_size, ratio], axis=1)
    columns = jnp.broadcast_to(rows, (128, 128)).T
    step_size, ratio = columns[0:64, 0:1], columns[64:128, 0:1]
    outs = (out0, out1, out2)
    copies = []
    for part in range(4):
        here = pl.ds(16 * part, 16)
        step, beta = step_size[16 * part : 16 * part + 16], ratio[16 * part : 16 * part + 16]
        direction = direction_ref[here, :]
        new_residual = residual_ref[here, :] - step * image_ref[here, :]
        held[0, here, :] = solution_ref[here, :] + step * direction
        held[1, here, :] = new_residual
        held[2, here, :] = new_residual + beta * direction
        for n in range(3):
            copy = pltpu.make_async_copy(
                held.at[n, here, :], outs[n].at[here, :], sems.at[3 * part + n]
            )
            copy.start()
            copies.append(copy)
    for copy in copies:
        copy.wait()


def call(kernel, outs, specs, *operands, scratch=(), flops=0, out_spec=VMEM):
    shapes = [jax.ShapeDtypeStruct(shape, dtype) for shape, dtype in outs]
    size = sum(o.size * o.dtype.itemsize for o in operands)
    size += sum(s.size * s.dtype.itemsize for s in shapes)
    single = len(shapes) == 1
    return pl.pallas_call(
        kernel,
        out_shape=shapes[0] if single else shapes,
        in_specs=specs,
        out_specs=out_spec if single else [out_spec] * len(shapes),
        scratch_shapes=list(scratch),
        compiler_params=pltpu.CompilerParams(vmem_limit_bytes=32 * 2**20),
        cost_estimate=pl.CostEstimate(flops=flops, bytes_accessed=size, transcendentals=0),
    )(*operands)


def meets(mine):
    apart = jnp.bitwise_xor(jnp.arange(16, dtype=jnp.int32)[:, None], mine)
    low = jnp.left_shift(1, jnp.arange(4, dtype=jnp.int32))[None, :]
    return (apart >= low) & (apart < 2 * low)


def local(
    features, lengthscale, signal_var, noise_var, factors, gains, solution, residual, direction
):
    core = lax.axis_index("core")
    place = core.astype(jnp.int32).reshape(1)

    projection = jnp.einsum(
        "cp,lpr->lcr", direction.astype(BF), factors, preferred_element_type=F32
    ).astype(BF)
    near_meets = meets(lax.axis_index(CHIP) ^ 15).reshape(16, 1, 4, 1, 1)
    far_meets = meets(lax.axis_index("z") ^ 8).reshape(16, 4, 1, 1)
    near = projection[:4].reshape(4, 2, 32, 128).transpose(1, 0, 2, 3)[None]
    near = jnp.sum(jnp.where(near_meets, near, 0.0).astype(F32), axis=2).astype(BF)
    far = projection[4:].reshape(4, 2, 32, 128).transpose(2, 0, 1, 3)
    sent = jnp.concatenate([near.reshape(32, 32, 128), far.reshape(32, 8, 128)], axis=1)
    got = lax.all_to_all(sent, LEAF, 0, 0, tiled=True, axis_index_groups=[LEAVES])

    own = jnp.concatenate([features] + parts_of(lax.optimization_barrier(direction), 2), axis=0)
    other = lax.ppermute(own, "core", SWAP)
    signal, noise = signal_var.reshape(1, 1), noise_var.reshape(1, 1)
    rate = (LOG2E / (lengthscale * lengthscale))[:, None]
    leaf = leaf_term(signal, rate, own, own)
    got, leaf = lax.optimization_barrier((got, leaf))

    plane_sum = jnp.sum(got[:, 32:].astype(F32), axis=0).reshape(1, 4, 2, 128)
    far = jnp.sum(jnp.where(far_meets, plane_sum, 0.0), axis=1).astype(BF)
    far = lax.all_to_all(far, "z", 0, 0, tiled=True, axis_index_groups=[PLANES])

    near = jnp.sum(got[:, :32].astype(F32).reshape(16, 2, 1, 32, 128), axis=1)
    near = jnp.sum(jnp.where(near_meets.reshape(16, 4, 1, 1), near, 0.0), axis=0)
    near = (gains[:4, None, :] * near).astype(BF)
    near_other = lax.ppermute(near, "core", SWAP)
    leaf = leaf_term(signal, rate, own, other, leaf)
    base = call(
        near_kernel, [((64, 1024), F32)], [SMEM] + [VMEM] * 6,
        place, noise, near, near_other, factors, leaf, direction, flops=2**26,
    )
    far, base = lax.optimization_barrier((far, base))

    far = jnp.sum(jnp.where(far_meets, far.astype(F32)[:, None], 0.0), axis=0)
    far = (gains[4:, None, :] * far).astype(BF).reshape(1, 8, 128)
    far = lax.all_to_all(jnp.broadcast_to(far, (32, 8, 128)), LEAF, 0, 0, tiled=True, axis_index_groups=[LEAVES])
    far = far.reshape(32, 4, 2, 128).transpose(1, 2, 0, 3).reshape(4, 64, 128)

    image, stats = call(
        image_kernel, [((64, 1024), F32), ((16, 1, 256), F32)],
        [VMEM] * 5,
        far, factors, base, direction, residual, flops=2**26,
    )
    stats = lax.all_to_all(stats, CHIP, 0, 0, tiled=True, axis_index_groups=[SQUARE]).sum(0)
    stats = jnp.broadcast_to(stats[None], (32, 1, 256))
    stats = lax.all_to_all(stats, ("core", "z"), 0, 0, tiled=True, axis_index_groups=[COLUMN])
    return call(
        step_kernel, [(direction.shape, F32)] * 3, [VMEM] * 5,
        stats, solution, residual, direction, image,
        scratch=[pltpu.VMEM((3,) + direction.shape, F32), pltpu.SemaphoreType.DMA((12,))],
        out_spec=HBM,
    )


def solution(mesh):
    fine = Mesh(mesh.devices.reshape(4, 4, 2, 16), ("x", "y", "core", "z"))
    points = P(None, ("z", "x", "y", "core"))
    return jax.shard_map(
        local,
        mesh=fine,
        in_specs=(
            points,
            P(),
            P(),
            P(),
            P(None, ("z", "x", "y", "core"), None),
            P(),
            points,
            points,
            points,
        ),
        out_specs=(points, points, points),
        check_vma=False,
    )
```

```python
import jax
import jax.numpy as jnp
import numpy as np
from jax import lax
from jax.experimental import pallas as pl
from jax.experimental.pallas import tpu as pltpu
from jax.sharding import Mesh, PartitionSpec as P

LOG2E = 1.4426950408889634
CHIP = ("x", "y")
LEAF = ("x", "y", "core")
ROW = ("y", "core")
VMEM = pl.BlockSpec(memory_space=pltpu.VMEM)
SMEM = pl.BlockSpec(memory_space=pltpu.SMEM)
HBM = pl.BlockSpec(memory_space=pltpu.HBM)
SWAP = [(0, 1), (1, 0)]
PLANES = [z ^ 8 for z in range(16)]
COLUMN = [16 * core + z for core in (1, 0) for z in PLANES]
LEAVES = [leaf ^ 30 for leaf in range(32)]
SQUARE = [chip ^ 15 for chip in range(16)]
BF = jnp.bfloat16
F32 = jnp.float32


def parts_of(value, count):
    parts = []
    for _ in range(count):
        part = value.astype(BF)
        parts.append(part)
        value = value - part.astype(F32)
    return parts


def leaf_kernel(signal_ref, rate_ref, own_ref, other_ref, *refs):
    out_ref = refs[-1]
    points = own_ref.shape[1]
    rate = rate_ref[...]
    row = lax.broadcasted_iota(jnp.int32, (16, points), 0)
    ones = jnp.where(row < 3, 1.0, 0.0).astype(BF)

    def prepared(ref):
        feat = ref[0:64, :]
        wide = feat.astype(F32)
        scaled = wide * rate
        half = -0.5 * jnp.sum(wide * scaled, axis=0, keepdims=True)
        one, two, three = [part.astype(F32) for part in parts_of(half, 3)]
        halves = jnp.where(row == 0, one, jnp.where(row == 1, two, jnp.where(row == 2, three, 0.0)))
        return feat, scaled, halves.astype(BF)

    _, scaled, halves = prepared(own_ref)
    feat, _, other_halves = prepared(other_ref)
    left = jnp.concatenate(parts_of(scaled, 3) + [halves, ones], axis=0).T
    right = jnp.concatenate([feat, feat, feat, ones, other_halves], axis=0)
    value = other_ref[64:192, :]
    dims = (((1,), (1,)), ((), ()))
    tile = 256
    for start in range(0, points, tile):
        here = slice(start, start + tile)
        power = jnp.dot(left[here], right, preferred_element_type=F32)
        high, low = parts_of(jnp.exp2(power), 2)
        both = lax.dot_general(high, value, dims, preferred_element_type=F32).T
        rest = lax.dot_general(low, value[0:64], dims, preferred_element_type=F32).T
        result = signal_ref[...] * (both[0:64] + both[64:128] + rest)
        if len(refs) > 1:
            result += refs[0][:, here]
        out_ref[:, here] = result


def leaf_term(signal, rate, own, other, *base):
    return pl.pallas_call(
        leaf_kernel,
        out_shape=jax.ShapeDtypeStruct((64, own.shape[1]), F32),
        in_specs=[VMEM] * (4 + len(base)),
        out_specs=VMEM,
        compiler_params=pltpu.CompilerParams(vmem_limit_bytes=40 * 2**20),
        cost_estimate=pl.CostEstimate(
            flops=2 * 1024 * 1024 * 256 * 3, bytes_accessed=2**20, transcendentals=1024 * 1024
        ),
    )(signal, rate, own, other, *base)


def image_kernel(
    place_ref,
    noise_ref,
    near_ref,
    near_other_ref,
    far_ref,
    factors_ref,
    leaf_ref,
    direction_ref,
    residual_ref,
    image_ref,
    stats_ref,
):
    first = place_ref[0] == 0
    levels = []
    for k in range(4):
        own, other = near_ref[k].astype(F32), near_other_ref[k].astype(F32)
        low = jnp.where(first, own, other)
        high = jnp.where(first, other, own)
        levels.append(jnp.concatenate([low, high], axis=0).astype(BF))
    levels += [far_ref[k] for k in range(4)]
    pairs = [jnp.concatenate(levels[k : k + 2], axis=1) for k in range(0, 8, 2)]
    points = direction_ref.shape[1]
    tile = 256
    sums = [jnp.zeros((64, 128), F32) for _ in range(4)]
    for start in range(0, points, tile):
        here = slice(start, start + tile)
        direction, residual = direction_ref[:, here], residual_ref[:, here]
        image = noise_ref[...] * direction + leaf_ref[:, here]
        for k in range(0, 8, 2):
            basis = jnp.concatenate([factors_ref[k, here, :], factors_ref[k + 1, here, :]], axis=1)
            image += lax.dot_general(
                pairs[k // 2], basis, (((1,), (1,)), ((), ())), preferred_element_type=F32
            )
        image_ref[:, here] = image
        products = [residual * residual, direction * image, residual * image, image * image]
        for n, product in enumerate(products):
            for lane in range(0, tile, 128):
                sums[n] += product[:, lane : lane + 128]
    row = jnp.sum(jnp.concatenate(sums, axis=0).T, axis=0, keepdims=True)
    for to in range(16):
        stats_ref[to] = row


def step_kernel(
    stats_ref, solution_ref, residual_ref, direction_ref, image_ref, out0, out1, out2, held, sems
):
    stats = stats_ref[0]
    for source in range(1, 32):
        stats += stats_ref[source]
    norm_now, curvature, cross, square = [stats[:, 64 * n : 64 * n + 64] for n in range(4)]
    step_size = norm_now / curvature
    norm_next = jnp.maximum(norm_now + step_size * (step_size * square - 2.0 * cross), 0.0)
    ratio = norm_next / norm_now
    rows = jnp.concatenate([step_size, ratio], axis=1)
    columns = jnp.broadcast_to(rows, (128, 128)).T
    step_size, ratio = columns[0:64, 0:1], columns[64:128, 0:1]
    outs = (out0, out1, out2)
    copies = []
    for part in range(4):
        here = pl.ds(16 * part, 16)
        step, beta = step_size[16 * part : 16 * part + 16], ratio[16 * part : 16 * part + 16]
        direction = direction_ref[here, :]
        new_residual = residual_ref[here, :] - step * image_ref[here, :]
        held[0, here, :] = solution_ref[here, :] + step * direction
        held[1, here, :] = new_residual
        held[2, here, :] = new_residual + beta * direction
        for n in range(3):
            copy = pltpu.make_async_copy(
                held.at[n, here, :], outs[n].at[here, :], sems.at[3 * part + n]
            )
            copy.start()
            copies.append(copy)
    for copy in copies:
        copy.wait()


def call(kernel, outs, specs, *operands, scratch=(), flops=0, out_spec=VMEM):
    shapes = [jax.ShapeDtypeStruct(shape, dtype) for shape, dtype in outs]
    size = sum(o.size * o.dtype.itemsize for o in operands)
    size += sum(s.size * s.dtype.itemsize for s in shapes)
    single = len(shapes) == 1
    return pl.pallas_call(
        kernel,
        out_shape=shapes[0] if single else shapes,
        in_specs=specs,
        out_specs=out_spec if single else [out_spec] * len(shapes),
        scratch_shapes=list(scratch),
        compiler_params=pltpu.CompilerParams(vmem_limit_bytes=32 * 2**20),
        cost_estimate=pl.CostEstimate(flops=flops, bytes_accessed=size, transcendentals=0),
    )(*operands)


def meets(mine):
    apart = jnp.bitwise_xor(jnp.arange(16, dtype=jnp.int32)[:, None], mine)
    low = jnp.left_shift(1, jnp.arange(4, dtype=jnp.int32))[None, :]
    return (apart >= low) & (apart < 2 * low)


def local(
    features, lengthscale, signal_var, noise_var, factors, gains, solution, residual, direction
):
    core = lax.axis_index("core")
    place = core.astype(jnp.int32).reshape(1)

    projection = jnp.einsum(
        "cp,lpr->lcr", direction.astype(BF), factors, preferred_element_type=F32
    ).astype(BF)
    near_meets = meets(lax.axis_index(CHIP) ^ 15).reshape(16, 1, 4, 1, 1)
    far_meets = meets(lax.axis_index("z") ^ 8).reshape(16, 4, 1, 1)
    near = projection[:4].reshape(4, 2, 32, 128).transpose(1, 0, 2, 3)[None]
    near = jnp.sum(jnp.where(near_meets, near, 0.0).astype(F32), axis=2).astype(BF)
    far = projection[4:].reshape(4, 2, 32, 128).transpose(2, 0, 1, 3)
    sent = jnp.concatenate([near.reshape(32, 32, 128), far.reshape(32, 8, 128)], axis=1)
    got = lax.all_to_all(sent, LEAF, 0, 0, tiled=True, axis_index_groups=[LEAVES])

    own = jnp.concatenate([features] + parts_of(lax.optimization_barrier(direction), 2), axis=0)
    other = lax.ppermute(own, "core", SWAP)
    signal, noise = signal_var.reshape(1, 1), noise_var.reshape(1, 1)
    rate = (LOG2E / (lengthscale * lengthscale))[:, None]
    leaf = leaf_term(signal, rate, own, own)
    got, leaf = lax.optimization_barrier((got, leaf))
    leaf = leaf_term(signal, rate, own, other, leaf)

    plane_sum = jnp.sum(got[:, 32:].astype(F32), axis=0).reshape(1, 4, 2, 128)
    far = jnp.sum(jnp.where(far_meets, plane_sum, 0.0), axis=1).astype(BF)
    far = lax.all_to_all(far, "z", 0, 0, tiled=True, axis_index_groups=[PLANES])

    near = jnp.sum(got[:, :32].astype(F32).reshape(16, 2, 1, 32, 128), axis=1)
    near = jnp.sum(jnp.where(near_meets.reshape(16, 4, 1, 1), near, 0.0), axis=0)
    near = (gains[:4, None, :] * near).astype(BF)
    near_other = lax.ppermute(near, "core", SWAP)

    far = jnp.sum(jnp.where(far_meets, far.astype(F32)[:, None], 0.0), axis=0)
    far = (gains[4:, None, :] * far).astype(BF).reshape(1, 8, 128)
    far = lax.all_to_all(jnp.broadcast_to(far, (32, 8, 128)), LEAF, 0, 0, tiled=True, axis_index_groups=[LEAVES])
    far = far.reshape(32, 4, 2, 128).transpose(1, 2, 0, 3).reshape(4, 64, 128)

    image, stats = call(
        image_kernel, [((64, 1024), F32), ((16, 1, 256), F32)],
        [SMEM] + [VMEM] * 8,
        place, noise, near, near_other, far, factors, leaf, direction, residual, flops=2**27,
    )
    stats = lax.all_to_all(stats, CHIP, 0, 0, tiled=True, axis_index_groups=[SQUARE]).sum(0)
    stats = jnp.broadcast_to(stats[None], (32, 1, 256))
    stats = lax.all_to_all(stats, ("core", "z"), 0, 0, tiled=True, axis_index_groups=[COLUMN])
    return call(
        step_kernel, [(direction.shape, F32)] * 3, [VMEM] * 5,
        stats, solution, residual, direction, image,
        scratch=[pltpu.VMEM((3,) + direction.shape, F32), pltpu.SemaphoreType.DMA((12,))],
        out_spec=HBM,
    )


def solution(mesh):
    fine = Mesh(mesh.devices.reshape(4, 4, 2, 16), ("x", "y", "core", "z"))
    points = P(None, ("z", "x", "y", "core"))
    return jax.shard_map(
        local,
        mesh=fine,
        in_specs=(
            points,
            P(),
            P(),
            P(),
            P(None, ("z", "x", "y", "core"), None),
            P(),
            points,
            points,
            points,
        ),
        out_specs=(points, points, points),
        check_vma=False,
    )
```

```python
import jax
import jax.numpy as jnp
import numpy as np
from jax import lax
from jax.experimental import pallas as pl
from jax.experimental.pallas import tpu as pltpu
from jax.sharding import Mesh, PartitionSpec as P

LOG2E = 1.4426950408889634
CHIP = ("x", "y")
LEAF = ("x", "y", "core")
ROW = ("y", "core")
VMEM = pl.BlockSpec(memory_space=pltpu.VMEM)
SMEM = pl.BlockSpec(memory_space=pltpu.SMEM)
HBM = pl.BlockSpec(memory_space=pltpu.HBM)
SWAP = [(0, 1), (1, 0)]
PLANES = [(8 - slot) % 16 for slot in range(16)]
COLUMN = [24, 16, 31, 17, 30, 18, 29, 19, 28, 20, 27, 21, 26, 22, 25, 23, 8, 0, 15, 1, 14, 2, 13, 3, 12, 4, 11, 5, 10, 6, 9, 7]
CHIPS = [15, 14, 13, 12, 11, 10, 9, 8, 7, 6, 5, 4, 3, 2, 1, 0]
LEAVES = [30, 31, 28, 29, 26, 27, 24, 25, 22, 23, 20, 21, 18, 19, 16, 17, 14, 15, 12, 13, 10, 11, 8, 9, 6, 7, 4, 5, 2, 3, 0, 1]
SQUARE = [15, 14, 13, 12, 11, 10, 9, 8, 7, 6, 5, 4, 3, 2, 1, 0]
BF = jnp.bfloat16
F32 = jnp.float32


def parts_of(value, count):
    parts = []
    for _ in range(count):
        part = value.astype(BF)
        parts.append(part)
        value = value - part.astype(F32)
    return parts


def leaf_kernel(signal_ref, rate_ref, own_ref, other_ref, *refs):
    out_ref = refs[-1]
    points = own_ref.shape[1]
    rate = rate_ref[...]
    row = lax.broadcasted_iota(jnp.int32, (16, points), 0)
    ones = jnp.where(row < 3, 1.0, 0.0).astype(BF)

    def prepared(ref):
        feat = ref[0:64, :]
        wide = feat.astype(F32)
        scaled = wide * rate
        half = -0.5 * jnp.sum(wide * scaled, axis=0, keepdims=True)
        one, two, three = [part.astype(F32) for part in parts_of(half, 3)]
        halves = jnp.where(row == 0, one, jnp.where(row == 1, two, jnp.where(row == 2, three, 0.0)))
        return feat, scaled, halves.astype(BF)

    _, scaled, halves = prepared(own_ref)
    feat, _, other_halves = prepared(other_ref)
    left = jnp.concatenate(parts_of(scaled, 3) + [halves, ones], axis=0).T
    right = jnp.concatenate([feat, feat, feat, ones, other_halves], axis=0)
    value = other_ref[64:192, :]
    dims = (((1,), (1,)), ((), ()))
    tile = 256
    for start in range(0, points, tile):
        here = slice(start, start + tile)
        power = jnp.dot(left[here], right, preferred_element_type=F32)
        high, low = parts_of(jnp.exp2(power), 2)
        both = lax.dot_general(high, value, dims, preferred_element_type=F32).T
        rest = lax.dot_general(low, value[0:64], dims, preferred_element_type=F32).T
        result = signal_ref[0] * (both[0:64] + both[64:128] + rest)
        if len(refs) > 1:
            result += refs[0][:, here]
        out_ref[:, here] = result


def leaf_term(signal, rate, own, other, *base):
    return pl.pallas_call(
        leaf_kernel,
        out_shape=jax.ShapeDtypeStruct((64, own.shape[1]), F32),
        in_specs=[SMEM] + [VMEM] * (3 + len(base)),
        out_specs=VMEM,
        compiler_params=pltpu.CompilerParams(vmem_limit_bytes=40 * 2**20),
        cost_estimate=pl.CostEstimate(
            flops=2 * 1024 * 1024 * 256 * 3, bytes_accessed=2**20, transcendentals=1024 * 1024
        ),
    )(signal, rate, own, other, *base)


def image_kernel(
    place_ref,
    noise_ref,
    near_ref,
    near_other_ref,
    far_ref,
    factors_ref,
    leaf_ref,
    direction_ref,
    residual_ref,
    image_ref,
    stats_ref,
):
    first = place_ref[0] == 0
    levels = []
    for k in range(4):
        own, other = near_ref[k].astype(F32), near_other_ref[k].astype(F32)
        low = jnp.where(first, own, other)
        high = jnp.where(first, other, own)
        levels.append(jnp.concatenate([low, high], axis=0).astype(BF))
    levels += [far_ref[k] for k in range(4)]
    pairs = [jnp.concatenate(levels[k : k + 2], axis=1) for k in range(0, 8, 2)]
    points = direction_ref.shape[1]
    tile = 256
    sums = [jnp.zeros((64, 128), F32) for _ in range(4)]
    for start in range(0, points, tile):
        here = slice(start, start + tile)
        direction, residual = direction_ref[:, here], residual_ref[:, here]
        image = noise_ref[0] * direction + leaf_ref[:, here]
        for k in range(0, 8, 2):
            basis = jnp.concatenate([factors_ref[k, here, :], factors_ref[k + 1, here, :]], axis=1)
            image += lax.dot_general(
                pairs[k // 2], basis, (((1,), (1,)), ((), ())), preferred_element_type=F32
            )
        image_ref[:, here] = image
        products = [residual * residual, direction * image, residual * image, image * image]
        for n, product in enumerate(products):
            for lane in range(0, tile, 128):
                sums[n] += product[:, lane : lane + 128]
    row = jnp.sum(jnp.concatenate(sums, axis=0).T, axis=0, keepdims=True)
    for to in range(16):
        stats_ref[to] = row


def step_kernel(
    stats_ref, solution_ref, residual_ref, direction_ref, image_ref, out0, out1, out2, held, sems
):
    stats = stats_ref[0]
    for source in range(1, 32):
        stats += stats_ref[source]
    norm_now, curvature, cross, square = [stats[:, 64 * n : 64 * n + 64] for n in range(4)]
    step_size = norm_now / curvature
    norm_next = jnp.maximum(norm_now + step_size * (step_size * square - 2.0 * cross), 0.0)
    ratio = norm_next / norm_now
    rows = jnp.concatenate([step_size, ratio], axis=1)
    columns = jnp.broadcast_to(rows, (128, 128)).T
    step_size, ratio = columns[0:64, 0:1], columns[64:128, 0:1]
    outs = (out0, out1, out2)
    copies = []
    for part in range(4):
        here = pl.ds(16 * part, 16)
        step, beta = step_size[16 * part : 16 * part + 16], ratio[16 * part : 16 * part + 16]
        direction = direction_ref[here, :]
        new_residual = residual_ref[here, :] - step * image_ref[here, :]
        held[0, here, :] = solution_ref[here, :] + step * direction
        held[1, here, :] = new_residual
        held[2, here, :] = new_residual + beta * direction
        for n in range(3):
            copy = pltpu.make_async_copy(
                held.at[n, here, :], outs[n].at[here, :], sems.at[3 * part + n]
            )
            copy.start()
            copies.append(copy)
    for copy in copies:
        copy.wait()


def call(kernel, outs, specs, *operands, scratch=(), flops=0, out_spec=VMEM):
    shapes = [jax.ShapeDtypeStruct(shape, dtype) for shape, dtype in outs]
    size = sum(o.size * o.dtype.itemsize for o in operands)
    size += sum(s.size * s.dtype.itemsize for s in shapes)
    single = len(shapes) == 1
    return pl.pallas_call(
        kernel,
        out_shape=shapes[0] if single else shapes,
        in_specs=specs,
        out_specs=out_spec if single else [out_spec] * len(shapes),
        scratch_shapes=list(scratch),
        compiler_params=pltpu.CompilerParams(vmem_limit_bytes=32 * 2**20),
        cost_estimate=pl.CostEstimate(flops=flops, bytes_accessed=size, transcendentals=0),
    )(*operands)


def meets(mine, first):
    slot = jnp.arange(16, dtype=jnp.int32)[:, None]
    apart = jnp.bitwise_xor(jnp.bitwise_and(first - slot, 15), mine)
    low = jnp.left_shift(1, jnp.arange(4, dtype=jnp.int32))[None, :]
    return (apart >= low) & (apart < 2 * low)


def local(
    features, lengthscale, signal_var, noise_var, factors, gains, solution, residual, direction
):
    core = lax.axis_index("core")
    place = core.astype(jnp.int32).reshape(1)

    projection = jnp.einsum(
        "cp,lpr->lcr", direction.astype(BF), factors, preferred_element_type=F32
    ).astype(BF)
    near_meets = meets(lax.axis_index(CHIP), 15).reshape(16, 1, 4, 1, 1)
    far_meets = meets(lax.axis_index("z"), 8).reshape(16, 4, 1, 1)
    near = projection[:4].reshape(4, 2, 32, 128).transpose(1, 0, 2, 3)[None]
    near = jnp.sum(jnp.where(near_meets, near, 0.0).astype(F32), axis=2).astype(BF)
    far = projection[4:].reshape(4, 2, 32, 128).transpose(2, 0, 1, 3)
    sent = jnp.concatenate([near.reshape(32, 32, 128), far.reshape(32, 8, 128)], axis=1)
    got = lax.all_to_all(sent, LEAF, 0, 0, tiled=True, axis_index_groups=[LEAVES])

    own = jnp.concatenate([features] + parts_of(lax.optimization_barrier(direction), 2), axis=0)
    other = lax.ppermute(own, "core", SWAP)
    rate = (LOG2E / (lengthscale * lengthscale))[:, None]
    leaf = leaf_term(signal_var, rate, own, own)
    got, leaf = lax.optimization_barrier((got, leaf))
    leaf = leaf_term(signal_var, rate, own, other, leaf)

    plane_sum = jnp.sum(got[:, 32:].astype(F32), axis=0).reshape(1, 4, 2, 128)
    far = jnp.sum(jnp.where(far_meets, plane_sum, 0.0), axis=1).astype(BF)
    far = lax.all_to_all(far, "z", 0, 0, tiled=True, axis_index_groups=[PLANES])

    near = jnp.sum(got[:, :32].astype(F32).reshape(16, 2, 1, 32, 128), axis=1)
    near = jnp.sum(jnp.where(near_meets.reshape(16, 4, 1, 1), near, 0.0), axis=0)
    near = (gains[:4, None, :] * near).astype(BF)
    near_other = lax.ppermute(near, "core", SWAP)

    far = jnp.sum(jnp.where(far_meets, far.astype(F32)[:, None], 0.0), axis=0)
    far = (gains[4:, None, :] * far).astype(BF).reshape(1, 8, 128)
    far = lax.all_to_all(jnp.broadcast_to(far, (32, 8, 128)), LEAF, 0, 0, tiled=True, axis_index_groups=[LEAVES])
    far = far.reshape(32, 4, 2, 128).transpose(1, 2, 0, 3).reshape(4, 64, 128)

    image, stats = call(
        image_kernel, [((64, 1024), F32), ((16, 1, 256), F32)],
        [SMEM, SMEM] + [VMEM] * 7,
        place, noise_var, near, near_other, far, factors, leaf, direction, residual, flops=2**27,
    )
    stats = lax.all_to_all(stats, CHIP, 0, 0, tiled=True, axis_index_groups=[SQUARE]).sum(0)
    stats = jnp.broadcast_to(stats[None], (32, 1, 256))
    stats = lax.all_to_all(stats, ("core", "z"), 0, 0, tiled=True, axis_index_groups=[COLUMN])
    return call(
        step_kernel, [(direction.shape, F32)] * 3, [VMEM] * 5,
        stats, solution, residual, direction, image,
        scratch=[pltpu.VMEM((3,) + direction.shape, F32), pltpu.SemaphoreType.DMA((12,))],
        out_spec=HBM,
    )


def solution(mesh):
    fine = Mesh(mesh.devices.reshape(4, 4, 2, 16), ("x", "y", "core", "z"))
    points = P(None, ("z", "x", "y", "core"))
    return jax.shard_map(
        local,
        mesh=fine,
        in_specs=(
            points,
            P(),
            P(),
            P(),
            P(None, ("z", "x", "y", "core"), None),
            P(),
            points,
            points,
            points,
        ),
        out_specs=(points, points, points),
        check_vma=False,
    )
```
